256 devices in a mesh: example: 64 (over x, z, core), feature: 4 (over y).
Axes of the slice: x: 4, y: 4, z: 8, core: 2. Of those that a mesh axis runs over, the one named last changes fastest.
Arguments:
- embeddings: bfloat16 [36864, 16384], P('example', 'feature'), may hold values from -16 to 16
- subspace: bfloat16 [16384, 128], P('feature'), may hold values from -0.046875 to 0.046875
- noise_levels: int32 [16384, 128], P('feature'), may hold values from -16 to 16
- targets: int32 [2048], replicated, may hold values from 0 to 16383
Outputs:
- embedding_grad: bfloat16 [36864, 16384], P('example', 'feature')
The draws below stay inside these ranges and needn't reach their ends.
All inputs are finite; a program needn't handle non-finite values.
Results may differ from the reference program's by a relative error of at most 0.0085.
Values may be sent and summed in bfloat16 or wider, within the bound.
A program may use at most 64 MiB of HBM per device.

```python
import jax
import jax.numpy as jnp
from jax import lax

F = 16384
K = 128
TARGETS = 2048
N = 36864


def plant(values, key, least, top_value):
    longest = values.shape.index(max(values.shape))
    spots = []
    for shift in (0, 1):
        where = [jax.random.randint(jax.random.fold_in(key, axis), (), 0, length) for axis, length in enumerate(values.shape)]
        where[longest] = (where[longest] + shift) % values.shape[longest]
        spots.append(tuple(where))
    return values.at[spots[0]].set(least).at[spots[1]].set(top_value)


def spiked(values, rng, source, target, blocks, factor):
    owner, partner = [(jnp.arange(values.shape[dim]) // (values.shape[dim] // blocks)).reshape([-1 if axis == dim else 1 for axis in range(values.ndim)]) for dim in (source, target)]
    chosen = jax.random.permutation(rng, blocks)[partner]
    strong = (owner == chosen) | (owner == (partner + blocks // 2) % blocks)
    return jnp.where(strong, factor * values, values)


def steps_of(key, extent, pieces, low, top_value):
    gain, own = 1.0, jax.random.fold_in(key, 6)
    for position, shards_of in pieces:
        steps = jnp.exp(jax.random.uniform(jax.random.fold_in(own, position), (shards_of,), jnp.float32, low / len(pieces), top_value / len(pieces)))
        gain = gain * jnp.repeat(steps, extent[position] // shards_of).reshape([-1 if axis == position else 1 for axis in range(len(extent))])
    return gain


def gaussian(rng, shape, scale, reach, split=(), kind=jnp.bfloat16):
    values = jax.random.normal(rng, shape, jnp.float32) * scale
    if len(split) > 0:
        values = steps_of(rng, shape, split, -0.22, 0.18) * values
    return jnp.clip(values, min=-reach, max=reach).astype(kind)


def bell_draw_with(own_key, shape, deviation, reach, pieces, heavy, held_as=jnp.bfloat16):
    values = deviation * jax.random.normal(own_key, shape, jnp.float32)
    if pieces:
        values = values * steps_of(own_key, shape, pieces, -0.22, 0.18)
    return jnp.clip(spiked(values, jax.random.fold_in(own_key, 3), *heavy), -reach, reach).astype(held_as)


def setup_inputs(seed: int = 0) -> dict:
    splits = jax.random.split(jax.random.key(seed), 5)
    embeddings = bell_draw_with(splits[0], (N, F), 1.0, 16.0, ((0, 64), (1, 4)), (0, 1, 64, 4.0))
    subspace = gaussian(splits[1], (F, K), F ** -0.5, 0.046875, ((0, 4),))
    noise_levels = plant(jax.random.randint(splits[2], (F, K), -16, 17), jax.random.fold_in(splits[2], 1), -16, 16).astype(jnp.int32)
    targets = plant(jax.random.randint(splits[3], (TARGETS,), 0, F), jax.random.fold_in(splits[3], 1), 0, F - 1).astype(jnp.int32)
    return {"embeddings": embeddings, "subspace": subspace, "noise_levels": noise_levels, "targets": targets}


NOISE_STEP = 1.0 / 4096.0
HIGH = lax.Precision.HIGHEST

def transposed(former, latter, precision=None):
    return lax.dot_general(former.astype(jnp.float32), latter.astype(jnp.float32), (((0,), (0,)), ((), ())), precision=precision, preferred_element_type=jnp.float32)

def by_columns(former, latter):
    return lax.dot_general(former.astype(jnp.float32), latter.astype(jnp.float32), (((1,), (1,)), ((), ())), preferred_element_type=jnp.float32)

def count_rows(targets, first, length):
    local = targets - first
    inside = (local >= 0) & (local < length)
    slots = jnp.where(inside, local, length).astype(jnp.int32)
    ones = jnp.ones(targets.shape, jnp.float32)
    return jax.ops.segment_sum(ones, slots, num_segments=length + 1)[:length]

def upper_factor(gram_matrix):
    return jnp.linalg.cholesky(gram_matrix).T

def reference(embeddings, subspace, noise_levels, targets):
    total_rows = embeddings.shape[0]
    projected = jnp.dot(embeddings.astype(jnp.float32), subspace.astype(jnp.float32), preferred_element_type=jnp.float32)
    projected_low = projected.astype(jnp.bfloat16)
    image = transposed(embeddings, projected_low) / total_rows + NOISE_STEP * noise_levels.astype(jnp.float32)
    row_counts = count_rows(targets, 0, image.shape[0])
    gram_matrix = transposed(image, image, HIGH)
    weighted = transposed(image * row_counts[:, None], image, HIGH)
    lower_factor = jnp.linalg.cholesky(gram_matrix)
    identity = jnp.eye(K, dtype=jnp.float32)
    inverse_factor = jax.scipy.linalg.solve_triangular(lower_factor, identity, lower=True)
    gram_inverse = jnp.dot(inverse_factor.T, inverse_factor, precision=HIGH)
    factor_grad = 2.0 * jnp.dot(jnp.dot(inverse_factor, weighted, precision=HIGH), gram_inverse, precision=HIGH)
    unused, pull_back = jax.vjp(upper_factor, gram_matrix)
    gram_grad = pull_back(factor_grad)[0]
    image_grad = jnp.dot(image, gram_grad + gram_grad.T, precision=HIGH) - 2.0 * row_counts[:, None] * jnp.dot(image, gram_inverse, precision=HIGH)
    grad_low = image_grad.astype(jnp.bfloat16)
    back_rows = jnp.dot(embeddings.astype(jnp.float32), grad_low.astype(jnp.float32), preferred_element_type=jnp.float32).astype(jnp.bfloat16)
    result = by_columns(projected_low, grad_low) + by_columns(back_rows, subspace)
    return result.astype(jnp.bfloat16)
```

```python
import functools

import jax
import jax.numpy as jnp
from jax import lax
from jax.experimental import pallas as pl
from jax.experimental.pallas import tpu as pltpu
from jax.sharding import PartitionSpec as P

MESH = pl.DeviceIdType.MESH
NOISE_STEP = 1.0 / 4096.0
HIGH = lax.Precision.HIGHEST
F32 = jnp.float32
BF16 = jnp.bfloat16
K = 128
H = K // 2
NT = (((1,), (1,)), ((), ()))


def far_first(n):
    return sorted(range(1, n), key=lambda d: -min(d, n - d))


def invert(a):
    lane = lax.broadcasted_iota(jnp.int32, (8, K), 1)
    row = lax.broadcasted_iota(jnp.int32, (8, K), 0)
    blocks = [a[8 * i : 8 * i + 8, :] for i in range(K // 8)]
    for p in range(K // 8):
        r = blocks[p]
        cols = [jnp.broadcast_to(r[:, 8 * p + j : 8 * p + j + 1], (8, K)) for j in range(8)]
        for j in range(8):
            k = 8 * p + j
            cj = cols[j]
            inv = 1.0 / jnp.broadcast_to(cj[j : j + 1, :], (8, K))
            y = jnp.where(lane == k, inv, jnp.broadcast_to(r[j : j + 1, :], (8, K)) * inv)
            r = jnp.where(row == j, y, jnp.where(lane == k, 0.0, r) - cj * y)
            for m in range(j + 1, 8):
                ym = jnp.broadcast_to(cols[m][j : j + 1, :], (8, K)) * inv
                cols[m] = jnp.where(row == j, ym, cols[m] - cj * ym)
        rows = [jnp.broadcast_to(r[j : j + 1, :], (8, K)) for j in range(8)]
        in_panel = (lane >= 8 * p) & (lane < 8 * p + 8)
        for i in range(K // 8):
            if i == p:
                continue
            b = blocks[i]
            total = jnp.where(in_panel, 0.0, b)
            for j in range(8):
                total = total - jnp.broadcast_to(b[:, 8 * p + j : 8 * p + j + 1], (8, K)) * rows[j]
            blocks[i] = total
        blocks[p] = r
    return jnp.concatenate(blocks, axis=0)


def split(v):
    hi = v.astype(BF16)
    return hi, (v - hi.astype(F32)).astype(BF16)


def kernel(X, Y, Z, total_rows, e_hbm, s_hbm, n_hbm, t_ref, pb_out, g_out,
           ebuf, sbuf, nbuf, ntr, cnt, cntb, e_sem, s_sem, n_sem, g_sem,
           ps, pr, plow, bs, br, blow, pt, ptp,
           u, cs, cr, xs, xr, zs, zr, imt, imn, itr,
           g, gr, gq, gpr, gfull, grad,
           p_ss, p_rs, pa_ss, pa_rs, b_ss, b_rs, ba_ss, ba_rs,
           c_ss, c_rs, x_ss, x_rs, z_ss, z_rs, h_ss, h_rs,
           gz_ss, gz_rs, gp_ss, gp_rs, ga_ss, ga_rs,
           az_ss, az_rs, ax_ss, ax_rs, ac_ss, ac_rs):
    R, W = ebuf.shape
    RC = R // Y
    CX = W // X
    GB = K // Z
    e = lax.axis_index("example")
    y = lax.axis_index("feature")
    x = e // (2 * Z)
    z = lax.rem(e // 2, Z)
    c = lax.rem(e, 2)

    def peer(dx=0, dy=0, dz=0, dc=0):
        px = lax.rem(x + dx, X)
        py = lax.rem(y + dy, Y)
        pz = lax.rem(z + dz, Z)
        pc = lax.rem(c + dc, 2)
        return ((px * Z + pz) * 2 + pc, py)

    def remote(src, dst, ss, rs, to):
        return pltpu.make_async_remote_copy(
            src_ref=src, dst_ref=dst, send_sem=ss, recv_sem=rs, device_id=to, device_id_type=MESH
        )

    sent = []

    def send(src, dst, ss, rs, to):
        copy = remote(src, dst, ss, rs, to)
        copy.start()
        sent.append(copy)
        return copy

    plane = [(dx, dy) for dx in range(X) for dy in range(Y) if (dx, dy) != (0, 0)]
    column = [(dz, dc) for dz in range(Z) for dc in range(2) if (dz, dc) != (0, 0)]

    s_copy = pltpu.make_async_copy(s_hbm, sbuf, s_sem)
    s_copy.start()
    y_order = far_first(Y) + [0]
    e_copies = {}
    for d in y_order:
        rows = pl.ds(pl.multiple_of(lax.rem(y + d, Y) * RC, 16), RC)
        e_copies[d] = pltpu.make_async_copy(e_hbm.at[rows], ebuf.at[rows], e_sem.at[d])
        e_copies[d].start()
    block = x * Z + z
    n_copy = pltpu.make_async_copy(n_hbm.at[pl.ds(pl.multiple_of(block * K, K), K)], nbuf, n_sem)
    n_copy.start()

    barrier = pltpu.get_barrier_semaphore()
    for dx, dy in plane:
        pl.semaphore_signal(barrier, inc=1, device_id=peer(dx=dx, dy=dy), device_id_type=MESH)
    for dz, dc in column:
        pl.semaphore_signal(barrier, inc=1, device_id=peer(dz=dz, dc=dc), device_id_type=MESH)

    s_copy.wait()
    first = True
    own = None
    for d in y_order:
        rows = pl.ds(pl.multiple_of(lax.rem(y + d, Y) * RC, 16), RC)
        e_copies[d].wait()
        part = jnp.dot(ebuf[rows, :], sbuf[...], preferred_element_type=F32)
        if d:
            ps[d - 1] = part.astype(BF16)
            if first:
                pl.semaphore_wait(barrier, len(plane) + len(column))
                first = False
            send(ps.at[d - 1], pr.at[d - 1], p_ss.at[d - 1], p_rs.at[d - 1], peer(dy=d))
        else:
            own = part

    t = t_ref[...]
    hi = lax.broadcasted_iota(jnp.int32, (W // K, t.shape[1]), 0) + y * (W // K)
    lo = lax.broadcasted_iota(jnp.int32, (K, t.shape[1]), 0)
    hot_hi = jnp.where(hi == t // K, 1.0, 0.0).astype(BF16)
    hot_lo = jnp.where(lo == lax.rem(t, K), 1.0, 0.0).astype(BF16)
    cnt[...] = lax.dot_general(hot_hi, hot_lo, NT, preferred_element_type=F32)
    n_copy.wait()
    ntr[...] = (NOISE_STEP * nbuf[...].astype(F32)).T

    my_rows = pl.ds(pl.multiple_of(y * RC, 16), RC)
    for d in range(1, Y):
        remote(ps.at[d - 1], pr.at[d - 1], p_ss.at[d - 1], p_rs.at[d - 1], peer(dy=d)).wait_recv()
        own = own + pr[d - 1].astype(F32)
    plow[my_rows, :] = own.astype(BF16)
    for d in far_first(Y):
        send(plow.at[my_rows], plow.at[my_rows], pa_ss.at[d - 1], pa_rs.at[d - 1], peer(dy=d))
    cnt_cols = lax.dot_general(hot_lo, hot_hi, NT, preferred_element_type=F32)
    for b in range(W // K):
        cntb[b] = jnp.broadcast_to(cnt_cols[:, b : b + 1], (K, K))
    for d in range(1, Y):
        rows = pl.ds(pl.multiple_of(lax.rem(y + Y - d, Y) * RC, 16), RC)
        remote(plow.at[rows], plow.at[rows], pa_ss.at[d - 1], pa_rs.at[d - 1], peer(dy=d)).wait_recv()

    pt[...] = plow[...].T
    ptp[0:H, :] = pt[pl.ds(pl.multiple_of(c * H, H), H), :]
    ptp[H:K, :] = pt[pl.ds(pl.multiple_of((1 - c) * H, H), H), :]
    x_order = far_first(X) + [0]

    def pass_on(d):
        remote(cs.at[d], cr.at[d], c_ss.at[d], c_rs.at[d], peer(dc=1)).wait_recv()
        v = u[d] + cr[d].astype(F32)
        if d:
            xs[d - 1] = v.astype(BF16)
            send(xs.at[d - 1], xr.at[d - 1], x_ss.at[d - 1], x_rs.at[d - 1], peer(dx=d))
        else:
            u[0] = v

    before = None
    for d in x_order:
        cols = pl.ds(pl.multiple_of(lax.rem(x + d, X) * CX, K), CX)
        part = jnp.dot(ptp[...], ebuf[:, cols], preferred_element_type=F32)
        cs[d] = part[H:K].astype(BF16)
        send(cs.at[d], cr.at[d], c_ss.at[d], c_rs.at[d], peer(dc=1))
        u[d] = part[0:H]
        if before is not None:
            pass_on(before)
        before = d
    pass_on(before)
    for d in range(1, X):
        remote(xs.at[d - 1], xr.at[d - 1], x_ss.at[d - 1], x_rs.at[d - 1], peer(dx=d)).wait_recv()
    total = None
    for d in far_first(Z) + [0]:
        cols = pl.ds(pl.multiple_of(lax.rem(z + d, Z) * K, K), K)
        v = u[0, :, cols]
        for dx in range(1, X):
            v = v + xr[dx - 1, :, cols].astype(F32)
        if d:
            zs[d - 1] = v.astype(BF16)
            send(zs.at[d - 1], zr.at[d - 1], z_ss.at[d - 1], z_rs.at[d - 1], peer(dz=d))
        else:
            total = v
    for d in range(1, Z):
        remote(zs.at[d - 1], zr.at[d - 1], z_ss.at[d - 1], z_rs.at[d - 1], peer(dz=d)).wait_recv()
        total = total + zr[d - 1].astype(F32)
    half = pl.ds(pl.multiple_of(c * H, H), H)
    other = pl.ds(pl.multiple_of((1 - c) * H, H), H)
    imt[half, :] = total / total_rows + ntr[half, :]
    send(imt.at[half], imt.at[half], h_ss, h_rs, peer(dc=1))
    remote(imt.at[other], imt.at[other], h_ss, h_rs, peer(dc=1)).wait_recv()

    im = imt[...]
    weight = jnp.where(c == 0, 1.0, cnt[pl.ds(block, 1), :])
    g[...] = lax.dot_general(im * weight, im, NT, precision=HIGH, preferred_element_type=F32)
    for d in far_first(Z):
        rows = pl.ds(pl.multiple_of(lax.rem(z + d, Z) * GB, 8), GB)
        send(g.at[rows], gr.at[d - 1], gz_ss.at[d - 1], gz_rs.at[d - 1], peer(dz=d))
    itr[...] = im.T
    imn[block, c] = itr[half, :]
    mine = pl.ds(pl.multiple_of(z * GB, 8), GB)
    v = g[mine, :]
    for d in range(1, Z):
        remote(gr.at[d - 1], gr.at[d - 1], gz_ss.at[d - 1], gz_rs.at[d - 1], peer(dz=d)).wait_recv()
        v = v + gr[d - 1]
    gq[...] = v
    for i, (dx, dy) in enumerate(plane):
        send(gq, gpr.at[i], gp_ss.at[i], gp_rs.at[i], peer(dx=dx, dy=dy))
    for i, (dx, dy) in enumerate(plane):
        remote(gq, gpr.at[i], gp_ss.at[i], gp_rs.at[i], peer(dx=dx, dy=dy)).wait_recv()
        v = v + gpr[i]
    gfull[c, mine, :] = v
    for i, (dz, dc) in enumerate(column):
        send(gfull.at[c, mine], gfull.at[c, mine], ga_ss.at[i], ga_rs.at[i], peer(dz=dz, dc=dc))

    for d in far_first(Z):
        send(imn.at[block, c], imn.at[block, c], az_ss.at[d - 1], az_rs.at[d - 1], peer(dz=d))

    for i, (dz, dc) in enumerate(column):
        sc = lax.rem(c + dc, 2)
        rows = pl.ds(pl.multiple_of(lax.rem(z + Z - dz, Z) * GB, 8), GB)
        remote(gfull.at[sc, rows], gfull.at[sc, rows], ga_ss.at[i], ga_rs.at[i], peer(dz=dz, dc=dc)).wait_recv()
    for d in range(1, Z):
        b = x * Z + lax.rem(z + Z - d, Z)
        remote(imn.at[b, c], imn.at[b, c], az_ss.at[d - 1], az_rs.at[d - 1], peer(dz=d)).wait_recv()
    slab = pl.ds(x * Z, Z)
    for d in far_first(X):
        send(imn.at[slab, c], imn.at[slab, c], ax_ss.at[d - 1], ax_rs.at[d - 1], peer(dx=d))
    send(imn.at[slab, c], imn.at[slab, c], ac_ss.at[0], ac_rs.at[0], peer(dc=1))

    inv = invert(gfull[0])
    mid = jnp.dot(inv, gfull[1], precision=HIGH, preferred_element_type=F32)
    mid = jnp.dot(mid, inv, precision=HIGH, preferred_element_type=F32)
    both_hi, both_lo = split(2.0 * jnp.concatenate([mid, inv], axis=1))

    for d in range(1, X):
        there = pl.ds(lax.rem(x + X - d, X) * Z, Z)
        remote(imn.at[there, c], imn.at[there, c], ax_ss.at[d - 1], ax_rs.at[d - 1], peer(dx=d)).wait_recv()
        send(imn.at[there, c], imn.at[there, c], ac_ss.at[d], ac_rs.at[d], peer(dc=1))
    for d in range(X):
        there = pl.ds(lax.rem(x + X - d, X) * Z, Z)
        remote(imn.at[there, 1 - c], imn.at[there, 1 - c], ac_ss.at[d], ac_rs.at[d], peer(dc=1)).wait_recv()

    for b in range(W // K):
        a_hi, a_lo = split(imn[b].reshape(K, K))
        v = jnp.dot(a_hi, both_hi, preferred_element_type=F32)
        v = v + jnp.dot(a_hi, both_lo, preferred_element_type=F32)
        v = v + jnp.dot(a_lo, both_hi, preferred_element_type=F32)
        grad[b * K : (b + 1) * K, :] = (v[:, :K] - cntb[b] * v[:, K:]).astype(BF16)
    g_copy = pltpu.make_async_copy(grad, g_out, g_sem)
    g_copy.start()

    for d in y_order:
        rows = pl.ds(pl.multiple_of(lax.rem(y + d, Y) * RC, 16), RC)
        part = jnp.dot(ebuf[rows, :], grad[...], preferred_element_type=F32)
        if d:
            bs[d - 1] = part.astype(BF16)
            send(bs.at[d - 1], br.at[d - 1], b_ss.at[d - 1], b_rs.at[d - 1], peer(dy=d))
        else:
            own = part
    for d in range(1, Y):
        remote(bs.at[d - 1], br.at[d - 1], b_ss.at[d - 1], b_rs.at[d - 1], peer(dy=d)).wait_recv()
        own = own + br[d - 1].astype(F32)
    blow[my_rows, :] = own.astype(BF16)
    for d in far_first(Y):
        send(blow.at[my_rows], blow.at[my_rows], ba_ss.at[d - 1], ba_rs.at[d - 1], peer(dy=d))
    pb_out[:, 0:K] = plow[...]
    for d in range(1, Y):
        rows = pl.ds(pl.multiple_of(lax.rem(y + Y - d, Y) * RC, 16), RC)
        remote(blow.at[rows], blow.at[rows], ba_ss.at[d - 1], ba_rs.at[d - 1], peer(dy=d)).wait_recv()
    pb_out[:, K:] = blow[...]

    for copy in sent:
        copy.wait_send()
    g_copy.wait()


def output_kernel(pb_ref, g_ref, s_ref, out_ref):
    both = jnp.concatenate([g_ref[...], s_ref[...]], axis=1)
    out_ref[...] = lax.dot_general(pb_ref[...], both, NT, preferred_element_type=F32).astype(BF16)


def make(X, Y, Z):
    def on_device(embeddings, subspace, noise_levels, targets):
        R, W = embeddings.shape
        RC, CX, B = R // Y, W // X, W // K
        dma = pltpu.SemaphoreType.DMA
        V = pltpu.VMEM
        any_spec = pl.BlockSpec(memory_space=pl.ANY)
        vmem_spec = pl.BlockSpec(memory_space=pltpu.VMEM)

        def sems(*counts):
            return [dma((n,)) for n in counts]

        pb, grad = pl.pallas_call(
            functools.partial(kernel, X, Y, Z, float(R * X * Z * 2)),
            out_shape=(jax.ShapeDtypeStruct((R, 2 * K), BF16), jax.ShapeDtypeStruct((W, K), BF16)),
            in_specs=[any_spec, any_spec, any_spec, vmem_spec],
            out_specs=(vmem_spec, any_spec),
            scratch_shapes=[
                V((R, W), BF16), V((W, K), BF16), V((K, K), jnp.int32), V((K, K), F32),
                V((B, K), F32), V((B, K, K), F32),
                dma((Y,)), dma, dma, dma,
                V((Y - 1, RC, K), BF16), V((Y - 1, RC, K), BF16), V((R, K), BF16),
                V((Y - 1, RC, K), BF16), V((Y - 1, RC, K), BF16), V((R, K), BF16),
                V((K, R), BF16), V((K, R), BF16),
                V((X, H, CX), F32), V((X, H, CX), BF16), V((X, H, CX), BF16),
                V((X - 1, H, CX), BF16), V((X - 1, H, CX), BF16),
                V((Z - 1, H, K), BF16), V((Z - 1, H, K), BF16),
                V((K, K), F32), V((B, 2, H, K), F32), V((K, K), F32),
                V((K, K), F32), V((Z - 1, K // Z, K), F32), V((K // Z, K), F32),
                V((X * Y - 1, K // Z, K), F32), V((2, K, K), F32), V((W, K), BF16),
                *sems(Y - 1, Y - 1, Y - 1, Y - 1, Y - 1, Y - 1, Y - 1, Y - 1),
                *sems(X, X, X - 1, X - 1, Z - 1, Z - 1), dma, dma,
                *sems(Z - 1, Z - 1, X * Y - 1, X * Y - 1, 2 * Z - 1, 2 * Z - 1),
                *sems(Z - 1, Z - 1, X - 1, X - 1, X, X),
            ],
            compiler_params=pltpu.CompilerParams(
                collective_id=0, has_side_effects=True, vmem_limit_bytes=50 * 2**20
            ),
        )(embeddings, subspace, noise_levels, targets.reshape(1, -1))

        tile = min(512, W)
        return pl.pallas_call(
            output_kernel,
            grid=(W // tile,),
            out_shape=jax.ShapeDtypeStruct((R, W), BF16),
            in_specs=[
                pl.BlockSpec((R, 2 * K), lambda i: (0, 0)),
                pl.BlockSpec((tile, K), lambda i: (i, 0)),
                pl.BlockSpec((tile, K), lambda i: (i, 0)),
            ],
            out_specs=pl.BlockSpec((R, tile), lambda i: (0, i)),
        )(pb, grad, subspace)

    return on_device


def solution(mesh, X=4, Z=8):
    in_specs = (P("example", "feature"), P("feature", None), P("feature", None), P())
    return jax.shard_map(
        make(X, mesh.shape["feature"], Z),
        mesh=mesh,
        in_specs=in_specs,
        out_specs=P("example", "feature"),
        check_vma=False,
    )
```
